32 devices in a mesh: runs: 2 (over x), fibre: 16 (over z, y, core).
Axes of the slice: x: 2, y: 2, z: 4, core: 2. Of those that a mesh axis runs over, the one named last changes fastest.
Arguments:
- records: bfloat16 [2048, 1600], P(('runs', 'fibre')), parts along dimension 0, may hold values from -6 to 6
- filter_taps: bfloat16 [9, 63], replicated, may hold values from -0.25 to 0.25
- segment_ids: int32 [2048], P('runs'), parts along dimension 0, may hold values from 0 to 7, never falling along the last dimension, each value on 1 to 256 neighbouring positions
Outputs:
- correlations: bfloat16 [2048, 5, 2048], P(('runs', 'fibre')), parts along dimension 0
- source_gathers: bfloat16 [2048, 512], P(('runs', 'fibre')), parts along dimension 0
The draws below stay inside these ranges and needn't reach their ends.
There are 2 independent parts, one for each index of `runs`. The reference program is written for one: setup_inputs(seed, part) draws one part's arguments, and reference() takes and returns one part's arrays. A program takes and returns all parts, laid end to end along the dimension named above; an argument that names none is the same for every part. Nothing has to cross between parts.
Inputs may be any that keep to these rules, and one draw needn't show every extreme that they name: `segment_ids`: segment numbers never fall along the fibre; each segment has 1 to 256 channels and one has exactly 256.
All inputs are finite; a program needn't handle non-finite values.
Results may differ from the reference program's by a relative error of at most 0.0073.
Values may be sent and summed in bfloat16 or wider, within the bound.
A program may use at most 128 MiB of HBM per device.

```python
import math
import jax
import jax.numpy as jnp
import numpy as np
from jax import lax

CB = 64
W = 4
F = 200
L = 400
TAPS = 63
SPAN = 9
LAGS = 32
BAND = 4
CHANNELS = 1024
SAMPLES = 1600
SEGCOUNT = 8
SEGMAX = 256
N_FIBRE = 16


def shard_levels(stream_key, shape, cuts, low, high):
    def one(axis_at, shards_of):
        steps = jax.random.uniform(jax.random.fold_in(jax.random.fold_in(stream_key, 6), axis_at), (shards_of,), jnp.float32, low / len(cuts), high / len(cuts))
        return jnp.repeat(jnp.exp(steps), shape[axis_at] // shards_of).reshape((-1,) + (1,) * (len(shape) - axis_at - 1))

    gain = one(*cuts[0])
    for cut in cuts[1:]:
        gain = gain * one(*cut)
    return gain


def length_profile(count, total, limit, skew):
    weights = [(1 << 20) // math.isqrt(standing ** skew) + 1 for standing in range(2, count + 1)]
    surplus, given = total - limit - (count - 1), [1] * (count - 1)
    while surplus > 0:
        free = [i for i in range(count - 1) if given[i] < limit]
        mass, remaining = sum([weights[i] for i in free]), surplus
        for i in free:
            extra = min(limit - given[i], max(1, remaining * weights[i] // mass), surplus)
            given[i] = given[i] + extra
            surplus = surplus - extra
    return np.array([limit] + given)


def uneven(stream_key, number_of, total, limit, slope):
    if number_of == 2:
        one = jax.random.randint(stream_key, (), max(1, total - limit), min(limit, total - 1) + 1)
        return jnp.stack([one, total - one])
    lengths = jnp.asarray(length_profile(number_of, total, limit, slope), jnp.int32)
    pairs = (number_of - 1) // 2
    giver, sink = lengths[1:1 + 2 * pairs:2], lengths[2:2 + 2 * pairs:2]
    room = jnp.minimum(giver - 1, limit - sink)
    shifted = jax.random.randint(jax.random.fold_in(stream_key, 1), (pairs,), 0, 1 << 20) % (room + 1)
    lengths = lengths.at[1:1 + 2 * pairs:2].set(giver - shifted).at[2:2 + 2 * pairs:2].set(sink + shifted)
    return lengths[jax.random.permutation(jax.random.fold_in(stream_key, 2), number_of)]


def noise(own_key, dims, width, most, split=(), held_as=jnp.bfloat16):
    drawn = jax.random.normal(own_key, dims, jnp.float32) * width
    if len(split) > 0:
        drawn = shard_levels(own_key, dims, split, -0.22, 0.18) * drawn
    return jnp.clip(drawn, min=-most, max=most).astype(held_as)


def setup_inputs(seed: int = 0, part: int = 0) -> dict:
    seeds = jax.random.split(jax.random.key(seed), 4)
    part_splits = jax.random.split(jax.random.fold_in(seeds[3], part), 4)
    records = noise(part_splits[0], (CHANNELS, SAMPLES), 1.0, 6.0, ((0, 16),))
    filter_taps = noise(seeds[1], (SPAN, TAPS), (SPAN * TAPS) ** -0.5, 0.25)
    segment_ids = jnp.searchsorted(jnp.cumsum(uneven(part_splits[2], SEGCOUNT, CHANNELS, SEGMAX, 2)), jnp.arange(CHANNELS), side="right").astype(jnp.int32)
    return dict(records=records, filter_taps=filter_taps, segment_ids=segment_ids)


def make_tables(filter_taps):
    extent = L + TAPS - 1
    out_time = jnp.arange(L).astype(jnp.int32)
    in_time = jnp.arange(extent).astype(jnp.int32)
    tap_index = out_time[None, :] - in_time[:, None] + (TAPS - 1)
    inside = (tap_index >= 0) & (tap_index < TAPS)
    safe_index = jnp.clip(tap_index, 0, TAPS - 1)
    toeplitz = jnp.where(inside[None], filter_taps[:, safe_index], jnp.zeros((), filter_taps.dtype))
    bin_index = jnp.arange(F).astype(jnp.int32)
    phase = (out_time[:, None] * bin_index[None, :] % L).astype(jnp.float32) * (2.0 * jnp.pi / L)
    window_taper = 0.5 - 0.5 * jnp.cos((out_time.astype(jnp.float32) + 0.5) * (2.0 * jnp.pi / L))
    dft_table = jnp.concatenate([window_taper[:, None] * jnp.cos(phase), -window_taper[:, None] * jnp.sin(phase)], axis=1).astype(jnp.bfloat16)
    lag_index = jnp.arange(LAGS).astype(jnp.int32) - LAGS // 2
    lag_phase = (bin_index[:, None] * lag_index[None, :] % L).astype(jnp.float32) * (2.0 * jnp.pi / L)
    scale = 1.0 / jnp.sqrt(jnp.float32(W * F))
    lag_table = (jnp.concatenate([jnp.cos(lag_phase), -jnp.sin(lag_phase)], axis=0) * scale).astype(jnp.bfloat16)
    return (toeplitz, dft_table, lag_table)

def spectra_of(padded, seg_local, toeplitz, dft_table):
    half_span = (SPAN - 1) // 2
    total = padded.shape[0]
    windows = padded.reshape(total, W, L)
    history = jnp.concatenate([jnp.zeros((total, 1, TAPS - 1), padded.dtype), windows[:, :-1, L - (TAPS - 1):]], axis=1)
    extended = jnp.concatenate([history, windows], axis=2)
    extent = L + TAPS - 1
    accum = jnp.zeros((CB * W, L), jnp.float32)
    for offset in range(SPAN):
        rows_in = extended[offset:offset + CB].reshape(CB * W, extent)
        product = jnp.dot(rows_in, toeplitz[offset], preferred_element_type=jnp.float32)
        keeping = (seg_local[offset:offset + CB] == seg_local[half_span:half_span + CB]).astype(jnp.float32)
        accum = accum + product * jnp.repeat(keeping, W)[:, None]
    filtered = accum.astype(jnp.bfloat16)
    spectrum = jnp.dot(filtered, dft_table, preferred_element_type=jnp.float32)
    power = lax.optimization_barrier(jnp.mean(spectrum * spectrum, axis=-1, keepdims=True))
    return (spectrum * lax.rsqrt(power + 1e-06)).astype(jnp.bfloat16).reshape(CB, W, 2 * F)

def correlate(own, partner, lag_table):
    count = partner.shape[0]
    own_four = own.reshape(CB, W, 2, F).astype(jnp.float32)
    other_four = partner.reshape(count, W, 2, F)
    rotated = jnp.stack([-other_four[:, :, 1], other_four[:, :, 0]], axis=2)
    stacked = jnp.concatenate([other_four, rotated], axis=0).astype(jnp.float32)
    cross = jnp.einsum('cwrf,dwrf->fcd', own_four, stacked).astype(jnp.bfloat16)
    parts = jnp.concatenate([cross[:, :, :count], cross[:, :, count:]], axis=0).astype(jnp.float32)
    return jnp.einsum('gcd,gl->cld', parts, lag_table.astype(jnp.float32))

def pair_block(own, partner, lag_table, keeping):
    total = correlate(own, partner, lag_table)
    return (total * keeping[:, None, :]).astype(jnp.bfloat16)

def reference(records, filter_taps, segment_ids):
    toeplitz, dft_table, lag_table = make_tables(filter_taps)
    half_span = (SPAN - 1) // 2
    padded_all = jnp.pad(records, ((half_span, half_span), (0, 0)))
    seg_padded = jnp.concatenate([jnp.full((half_span,), -1, jnp.int32), segment_ids.astype(jnp.int32), jnp.full((half_span + BAND * CB,), -1, jnp.int32)])

    def one_block(block):
        start = (block * CB).astype(jnp.int32)
        padded = lax.dynamic_slice_in_dim(padded_all, start, CB + 2 * half_span, 0)
        seg_local = lax.dynamic_slice_in_dim(seg_padded, start, CB + 2 * half_span, 0)
        return spectra_of(padded, seg_local, toeplitz, dft_table)
    blocks = jnp.arange(N_FIBRE).astype(jnp.int32)
    all_spectra = lax.map(one_block, blocks)
    sources = all_spectra[:, 0]
    extended = jnp.concatenate([all_spectra, jnp.zeros((BAND,) + all_spectra.shape[1:], all_spectra.dtype)], axis=0)

    def pairs(block):
        start = (block * CB).astype(jnp.int32)
        own_seg = lax.dynamic_slice_in_dim(seg_padded, start + half_span, CB, 0)
        own = lax.dynamic_index_in_dim(extended, block, 0, keepdims=False)
        results = []
        for offset in range(BAND + 1):
            partner = lax.dynamic_index_in_dim(extended, block + offset, 0, keepdims=False)
            partner_seg = lax.dynamic_slice_in_dim(seg_padded, start + offset * CB + half_span, CB, 0)
            keeping = (own_seg[:, None] == partner_seg[None, :]).astype(jnp.float32)
            results.append(pair_block(own, partner, lag_table, keeping))
        return jnp.stack(results, axis=1)

    def gathers(block):
        own = lax.dynamic_index_in_dim(extended, block, 0, keepdims=False)
        return correlate(own, sources, lag_table).astype(jnp.bfloat16)
    outcome = lax.map(pairs, blocks)
    source_out = lax.map(gathers, blocks)
    return (outcome.reshape(CHANNELS, BAND + 1, LAGS * CB), source_out.reshape(CHANNELS, LAGS * N_FIBRE))
```

```python
import functools

import jax
import jax.numpy as jnp
import numpy as np
from jax import lax
from jax.experimental import pallas as pl
from jax.experimental.pallas import tpu as pltpu
from jax.sharding import PartitionSpec as P

CB = 64
W = 4
F = 200
L = 400
TAPS = 63
SPAN = 9
LAGS = 32
BAND = 4

HALF = SPAN // 2
LANES = 128
PART = 256
WIDE = 2 * PART
KDIM = W * WIDE
TILE = 256
DEPTH = TILE + LANES
EDGE = 8


def tables():
    time = np.arange(L)
    bins = np.arange(F)
    phase = (time[:, None] * bins[None, :] % L) * (2.0 * np.pi / L)
    taper = 0.5 - 0.5 * np.cos((time + 0.5) * (2.0 * np.pi / L))
    slack = (L % LANES) * (W - 1)
    rows = slack + WIDE
    dft = np.zeros((rows, WIDE), np.float32)
    dft[slack : slack + L, :F] = taper[:, None] * np.cos(phase)
    dft[slack : slack + L, PART : PART + F] = -taper[:, None] * np.sin(phase)
    lag = np.arange(LAGS) - LAGS // 2
    lag_phase = (lag[:, None] * bins[None, :] % L) * (2.0 * np.pi / L)
    scale = 1.0 / np.sqrt(W * F)
    lags = np.zeros((2, LAGS, PART), np.float32)
    lags[0, :, :F] = np.cos(lag_phase) * scale
    lags[1, :, :F] = -np.sin(lag_phase) * scale
    lags = jnp.asarray(lags).astype(jnp.bfloat16).astype(jnp.float32)
    return jnp.asarray(dft).astype(jnp.bfloat16), lags


def column(row):
    across = lax.broadcasted_iota(jnp.int32, (CB, CB), 1)
    down = lax.broadcasted_iota(jnp.int32, (CB, CB), 0)
    return jnp.sum(jnp.where(across == down, row, 0.0), axis=1, keepdims=True)


def build_toeplitz(taps_ref, base, toep):
    base[...] = jnp.zeros_like(base)
    base[0:SPAN, 0:TAPS] = taps_ref[...].astype(jnp.float32)
    toep[...] = jnp.zeros_like(toep)
    for e in range(SPAN):
        rows = jnp.broadcast_to(base[e : e + 1, :], (LANES, 2 * LANES))
        near = pltpu.roll(rows, 0, 1, stride=1, stride_axis=0).astype(jnp.bfloat16)
        at = e * DEPTH
        toep[at : at + LANES, 0:LANES] = near[:, LANES:]
        toep[at + LANES : at + 2 * LANES, :] = near
        toep[at + 2 * LANES : at + 3 * LANES, LANES:] = near[:, :LANES]


def fill_segments(seg_ref, segcol):
    seg = seg_ref[...].astype(jnp.float32)
    segcol[0:EDGE] = jnp.broadcast_to(column(seg[0:1])[CB - EDGE :], (EDGE, LANES))
    segcol[EDGE : EDGE + CB] = jnp.broadcast_to(column(seg[1:2]), (CB, LANES))
    segcol[EDGE + CB :] = jnp.broadcast_to(column(seg[2:3])[:EDGE], (EDGE, LANES))


def filter_and_transform(xf, segcol, xs, toep, y, dft_ref, emit):
    blocks = xs.shape[0] // CB
    own = segcol[EDGE : EDGE + CB]
    for e in range(SPAN):
        lower = EDGE - HALF + e
        keep = segcol[lower : lower + CB] == own
        for j in range(xf.shape[1] // LANES):
            part = xf[lower : lower + CB, j * LANES : (j + 1) * LANES]
            part = jnp.where(keep, part, 0.0).astype(jnp.bfloat16)
            for b in range(blocks):
                k = j - b * (TILE // LANES)
                if 0 <= k < DEPTH // LANES:
                    at = e * DEPTH + k * LANES
                    xs[b * CB : (b + 1) * CB, at : at + LANES] = part
    out = jnp.dot(xs[...], toep[...], preferred_element_type=jnp.float32)
    out = out.astype(jnp.bfloat16)
    for b in range(blocks):
        y[:, b * TILE : (b + 1) * TILE] = out[b * CB : (b + 1) * CB]
    slack = L % LANES
    for w in range(W):
        first = w * (L - slack)
        top = slack * (W - 1 - w)
        raw = jnp.dot(
            y[:, first : first + WIDE],
            dft_ref[top : top + WIDE, :],
            preferred_element_type=jnp.float32,
        )
        power = jnp.sum(raw * raw, axis=-1, keepdims=True) * (1.0 / (2 * F))
        emit(w, raw * lax.rsqrt(power + 1e-06))


def spectra_kernel(low_ref, x_ref, high_ref, taps_ref, seg_ref, dft_ref, out_ref, base, toep, segcol, xf, xs, y):
    build_toeplitz(taps_ref, base, toep)
    fill_segments(seg_ref, segcol)
    xf[...] = jnp.zeros_like(xf)
    samples = x_ref.shape[1]
    edge = low_ref.shape[0]
    xf[0:EDGE, LANES : LANES + samples] = low_ref[edge - EDGE :].astype(jnp.float32)
    xf[EDGE : EDGE + CB, LANES : LANES + samples] = x_ref[...].astype(jnp.float32)
    xf[EDGE + CB :, LANES : LANES + samples] = high_ref[0:EDGE].astype(jnp.float32)

    def emit(w, value):
        out_ref[:, w * WIDE : (w + 1) * WIDE] = value.astype(jnp.bfloat16)

    filter_and_transform(xf, segcol, xs, toep, y, dft_ref, emit)


def rotate(own_ref, lag_ref, turned):
    def put(l, w, re, im):
        rows = slice(l * CB, (l + 1) * CB)
        turned[rows, w * WIDE : w * WIDE + PART] = re.astype(jnp.bfloat16)
        turned[rows, w * WIDE + PART : (w + 1) * WIDE] = im.astype(jnp.bfloat16)

    middle = LAGS // 2
    for w in range(W):
        re = own_ref[:, w * WIDE : w * WIDE + PART].astype(jnp.float32)
        im = own_ref[:, w * WIDE + PART : (w + 1) * WIDE].astype(jnp.float32)
        for l in range(middle + 1):
            cos, sin = lag_ref[0, l : l + 1], lag_ref[1, l : l + 1]
            a, b, c, d = re * cos, im * sin, im * cos, re * sin
            put(l, w, a + b, c - d)
            if 0 < l < middle:
                put(2 * middle - l, w, a - b, c + d)


def place(total, lags, first, keeps, corr_ref, n, src_ref):
    def at(l, lower, width):
        return total[(l - first) * CB : (l - first + 1) * CB, lower : lower + width]

    for l in range(first, first + lags, 2):
        for k in range(BAND + 1):
            pair = jnp.concatenate([at(l, k * CB, CB), at(l + 1, k * CB, CB)], axis=1)
            pair = jnp.where(keeps[k], pair, 0.0)
            corr_ref[k, :, l * CB : (l + 2) * CB] = pair.astype(jnp.bfloat16)
    lower = (BAND + 1) * CB
    gathers = jnp.concatenate([at(l, lower, n) for l in range(first, first + lags)], axis=1)
    src_ref[:, first * n : (first + lags) * n] = gathers.astype(jnp.bfloat16)


def pair_masks(seg_ref):
    seg = seg_ref[...].astype(jnp.float32)
    own = column(seg[1:2])
    keeps = []
    for k in range(BAND + 1):
        row = seg[1 + k : 2 + k]
        row = jnp.concatenate([row, row], axis=1)
        keeps.append(jnp.broadcast_to(own, (CB, 2 * CB)) == row)
    return keeps


def pairs_kernel(n, own_ref, other_ref, seg_ref, lag_ref, corr_ref, src_ref, turned):
    rotate(own_ref, lag_ref, turned)
    keeps = pair_masks(seg_ref)
    group = 8
    for first in range(0, LAGS, group):
        total = lax.dot_general(
            turned[first * CB : (first + group) * CB],
            other_ref[...],
            (((1,), (1,)), ((), ())),
            preferred_element_type=jnp.float32,
        )
        place(total, group, first, keeps, corr_ref, n, src_ref)


def per_device(records, filter_taps, segment_ids):
    n = lax.axis_size("fibre")
    me = lax.axis_index("fibre")
    samples = records.shape[1]
    dft, lags = tables()
    seg = jnp.pad(segment_ids.reshape(n, CB), ((1, BAND + 1), (0, 0)), constant_values=-1)
    seg = lax.dynamic_slice_in_dim(seg, me, BAND + 3, 0)
    up = [(i, i + 1) for i in range(n - 1)]
    low = lax.ppermute(records[CB - EDGE :], "fibre", up)
    high = lax.ppermute(records[:EDGE], "fibre", [(b, a) for a, b in up])
    blocks = -(-samples // TILE)
    vmem = pl.BlockSpec(memory_space=pltpu.VMEM)
    own = pl.pallas_call(
        spectra_kernel,
        out_shape=jax.ShapeDtypeStruct((CB, KDIM), jnp.bfloat16),
        in_specs=[vmem] * 6,
        out_specs=vmem,
        scratch_shapes=[
            pltpu.VMEM((16, 2 * LANES), jnp.float32),
            pltpu.VMEM((SPAN * DEPTH, TILE), jnp.bfloat16),
            pltpu.VMEM((CB + 2 * EDGE, LANES), jnp.float32),
            pltpu.VMEM((CB + 2 * EDGE, LANES + blocks * TILE), jnp.float32),
            pltpu.VMEM((blocks * CB, SPAN * DEPTH), jnp.bfloat16),
            pltpu.VMEM((CB, blocks * TILE), jnp.bfloat16),
        ],
        compiler_params=pltpu.CompilerParams(vmem_limit_bytes=32 << 20),
        name="spectra",
    )(low, records, high, filter_taps, seg, dft)
    parts = [own]
    for k in range(1, BAND + 1):
        parts.append(lax.ppermute(own, "fibre", [(i, i - k) for i in range(k, n)]))
    parts.append(lax.all_gather(own[:1], "fibre", axis=0, tiled=True))
    corr, src = pl.pallas_call(
        functools.partial(pairs_kernel, n),
        out_shape=(
            jax.ShapeDtypeStruct((BAND + 1, CB, LAGS * CB), jnp.bfloat16),
            jax.ShapeDtypeStruct((CB, LAGS * n), jnp.bfloat16),
        ),
        in_specs=[vmem] * 4,
        out_specs=(vmem, vmem),
        scratch_shapes=[pltpu.VMEM((LAGS * CB, KDIM), jnp.bfloat16)],
        compiler_params=pltpu.CompilerParams(vmem_limit_bytes=40 << 20),
        name="pairs",
    )(own, jnp.concatenate(parts, axis=0), seg, lags)
    return corr.transpose(1, 0, 2), src


def solution(mesh):
    return jax.shard_map(
        per_device,
        mesh=mesh,
        in_specs=(P(("runs", "fibre"), None), P(), P("runs")),
        out_specs=(P(("runs", "fibre"), None, None), P(("runs", "fibre"), None)),
        check_vma=False,
    )
```

```python
import functools

import jax
import jax.numpy as jnp
import numpy as np
from jax import lax
from jax.experimental import pallas as pl
from jax.experimental.pallas import tpu as pltpu
from jax.sharding import PartitionSpec as P

CB = 64
W = 4
F = 200
L = 400
TAPS = 63
SPAN = 9
LAGS = 32
BAND = 4

HALF = SPAN // 2
LANES = 128
PART = 256
WIDE = 2 * PART
KDIM = W * WIDE
TILE = 256
DEPTH = TILE + LANES
EDGE = 8
MESH = pl.DeviceIdType.MESH


def tables():
    time = np.arange(L)
    bins = np.arange(F)
    phase = (time[:, None] * bins[None, :] % L) * (2.0 * np.pi / L)
    taper = 0.5 - 0.5 * np.cos((time + 0.5) * (2.0 * np.pi / L))
    slack = (L % LANES) * (W - 1)
    rows = slack + WIDE
    dft = np.zeros((rows, WIDE), np.float32)
    dft[slack : slack + L, :F] = taper[:, None] * np.cos(phase)
    dft[slack : slack + L, PART : PART + F] = -taper[:, None] * np.sin(phase)
    lag = np.arange(LAGS) - LAGS // 2
    lag_phase = (lag[:, None] * bins[None, :] % L) * (2.0 * np.pi / L)
    scale = 1.0 / np.sqrt(W * F)
    lags = np.zeros((2, LAGS, PART), np.float32)
    lags[0, :, :F] = np.cos(lag_phase) * scale
    lags[1, :, :F] = -np.sin(lag_phase) * scale
    lags = jnp.asarray(lags).astype(jnp.bfloat16).astype(jnp.float32)
    return jnp.asarray(dft).astype(jnp.bfloat16), lags


def column(row):
    across = lax.broadcasted_iota(jnp.int32, (CB, CB), 1)
    down = lax.broadcasted_iota(jnp.int32, (CB, CB), 0)
    return jnp.sum(jnp.where(across == down, row, 0.0), axis=1, keepdims=True)


def build_toeplitz(taps_ref, base, toep):
    base[...] = jnp.zeros_like(base)
    base[0:SPAN, 0:TAPS] = taps_ref[...].astype(jnp.float32)
    toep[...] = jnp.zeros_like(toep)
    for e in range(SPAN):
        rows = jnp.broadcast_to(base[e : e + 1, :], (LANES, 2 * LANES))
        near = pltpu.roll(rows, 0, 1, stride=1, stride_axis=0).astype(jnp.bfloat16)
        at = e * DEPTH
        toep[at : at + LANES, 0:LANES] = near[:, LANES:]
        toep[at + LANES : at + 2 * LANES, :] = near
        toep[at + 2 * LANES : at + 3 * LANES, LANES:] = near[:, :LANES]


def fill_segments(seg_ref, segcol):
    seg = seg_ref[...].astype(jnp.float32)
    segcol[0:EDGE] = jnp.broadcast_to(column(seg[0:1])[CB - EDGE :], (EDGE, LANES))
    segcol[EDGE : EDGE + CB] = jnp.broadcast_to(column(seg[1:2]), (CB, LANES))
    segcol[EDGE + CB :] = jnp.broadcast_to(column(seg[2:3])[:EDGE], (EDGE, LANES))


def filter_and_transform(xf, segcol, xs, toep, y, dft_ref, emit):
    blocks = xs.shape[0] // CB
    own = segcol[EDGE : EDGE + CB]
    for e in range(SPAN):
        lower = EDGE - HALF + e
        keep = segcol[lower : lower + CB] == own
        for j in range(xf.shape[1] // LANES):
            part = xf[lower : lower + CB, j * LANES : (j + 1) * LANES]
            part = jnp.where(keep, part, 0.0).astype(jnp.bfloat16)
            for b in range(blocks):
                k = j - b * (TILE // LANES)
                if 0 <= k < DEPTH // LANES:
                    at = e * DEPTH + k * LANES
                    xs[b * CB : (b + 1) * CB, at : at + LANES] = part
    out = jnp.dot(xs[...], toep[...], preferred_element_type=jnp.float32)
    out = out.astype(jnp.bfloat16)
    for b in range(blocks):
        y[:, b * TILE : (b + 1) * TILE] = out[b * CB : (b + 1) * CB]
    slack = L % LANES
    for w in range(W):
        first = w * (L - slack)
        top = slack * (W - 1 - w)
        raw = jnp.dot(
            y[:, first : first + WIDE],
            dft_ref[top : top + WIDE, :],
            preferred_element_type=jnp.float32,
        )
        power = jnp.sum(raw * raw, axis=-1, keepdims=True) * (1.0 / (2 * F))
        emit(w, raw * lax.rsqrt(power + 1e-06))


def rotate(own_ref, lag_ref, turned):
    def put(l, w, re, im):
        rows = slice(l * CB, (l + 1) * CB)
        turned[rows, w * WIDE : w * WIDE + PART] = re.astype(jnp.bfloat16)
        turned[rows, w * WIDE + PART : (w + 1) * WIDE] = im.astype(jnp.bfloat16)

    middle = LAGS // 2
    for w in range(W):
        re = own_ref[:, w * WIDE : w * WIDE + PART].astype(jnp.float32)
        im = own_ref[:, w * WIDE + PART : (w + 1) * WIDE].astype(jnp.float32)
        for l in range(middle + 1):
            cos, sin = lag_ref[0, l : l + 1], lag_ref[1, l : l + 1]
            a, b, c, d = re * cos, im * sin, im * cos, re * sin
            put(l, w, a + b, c - d)
            if 0 < l < middle:
                put(2 * middle - l, w, a - b, c + d)


def place(total, lags, first, blocks, keeps, corr_ref, n, src_ref):
    def at(l, lower, width):
        return total[(l - first) * CB : (l - first + 1) * CB, lower : lower + width]

    for l in range(first, first + lags, 2):
        for i, k in enumerate(blocks):
            pair = jnp.concatenate([at(l, i * CB, CB), at(l + 1, i * CB, CB)], axis=1)
            pair = jnp.where(keeps[k], pair, 0.0)
            corr_ref[k, :, l * CB : (l + 2) * CB] = pair.astype(jnp.bfloat16)
    if src_ref is None:
        return
    lower = len(blocks) * CB
    gathers = jnp.concatenate([at(l, lower, n) for l in range(first, first + lags)], axis=1)
    src_ref[:, first * n : (first + lags) * n] = gathers.astype(jnp.bfloat16)


def pair_masks(seg_ref):
    seg = seg_ref[...].astype(jnp.float32)
    own = column(seg[1:2])
    keeps = []
    for k in range(BAND + 1):
        row = seg[1 + k : 2 + k]
        row = jnp.concatenate([row, row], axis=1)
        keeps.append(jnp.broadcast_to(own, (CB, 2 * CB)) == row)
    return keeps


def pair_products(n, turned, partner, blocks, keeps, corr_ref, src_ref):
    group = 8
    for first in range(0, LAGS, group):
        total = lax.dot_general(
            turned[first * CB : (first + group) * CB],
            partner,
            (((1,), (1,)), ((), ())),
            preferred_element_type=jnp.float32,
        )
        place(total, group, first, blocks, keeps, corr_ref, n, src_ref)


def kernel(
    n, x_ref, taps_ref, seg_ref, dft_ref, lag_ref, corr_ref, src_ref,
    base, toep, segcol, xf, xs, y, low, high, own, others, turned, row, row_tile, rows_in, rows_wide,
    halo_send, halo_recv, block_send, block_recv, row_send, row_recv,
):
    me = lax.axis_index("fibre")
    barrier = pltpu.get_barrier_semaphore()

    @pl.loop(1, n)
    def _(d):
        pl.semaphore_signal(barrier, inc=1, device_id={"fibre": lax.rem(me + d, n)}, device_id_type=MESH)

    build_toeplitz(taps_ref, base, toep)
    fill_segments(seg_ref, segcol)
    keeps = pair_masks(seg_ref)
    xf[...] = jnp.zeros_like(xf)
    samples = x_ref.shape[1]
    xf[EDGE : EDGE + CB, LANES : LANES + samples] = x_ref[...].astype(jnp.float32)
    halo = low.shape[0]
    pl.semaphore_wait(barrier, n - 1)

    def remote(source, target, send, recv, device):
        return pltpu.make_async_remote_copy(
            src_ref=source, dst_ref=target, send_sem=send, recv_sem=recv,
            device_id={"fibre": device}, device_id_type=MESH,
        )

    has_low, has_high = me > 0, me < n - 1
    to_low = remote(x_ref.at[0:halo], high, halo_send.at[0], halo_recv.at[0], me - 1)
    to_high = remote(x_ref.at[CB - halo : CB], low, halo_send.at[1], halo_recv.at[1], me + 1)
    pl.when(has_low)(to_low.start)
    pl.when(has_high)(to_high.start)

    @pl.when(has_high)
    def _():
        to_low.wait_recv()
        xf[EDGE + CB :, LANES : LANES + samples] = high[0:EDGE].astype(jnp.float32)

    @pl.when(has_low)
    def _():
        to_high.wait_recv()
        xf[0:EDGE, LANES : LANES + samples] = low[halo - EDGE :].astype(jnp.float32)

    def emit(w, value):
        own[:, w * WIDE : (w + 1) * WIDE] = value.astype(jnp.bfloat16)
        for j in range(WIDE // LANES):
            at = w * (WIDE // LANES) + j
            row[at : at + 1, :] = value[0:1, j * LANES : (j + 1) * LANES]

    filter_and_transform(xf, segcol, xs, toep, y, dft_ref, emit)

    def slot(k):
        return others.at[(k - 1) * CB : k * CB]

    def block_copy(source, k, sem, device):
        return remote(source, slot(k), block_send.at[sem], block_recv.at[k - 1], device)

    even = lax.rem(me, 2) == 0
    odd = lax.rem(me, 2) == 1
    to_two = block_copy(own, 2, 0, me - 2)
    to_four = block_copy(own, 4, 1, me - 4)
    own_down = block_copy(own, 1, 2, me - 1)
    two_down = block_copy(slot(2), 3, 3, me - 1)
    two_up = block_copy(slot(2), 1, 2, me + 1)
    four_up = block_copy(slot(4), 3, 3, me + 1)
    pl.when(me >= 2)(to_two.start)
    pl.when(me >= 4)(to_four.start)
    pl.when(odd)(own_down.start)
    row_tile[...] = row[...].astype(jnp.bfloat16)
    rows_in[me] = row_tile[...]

    def row_copy(d, at):
        return remote(row_tile, rows_in.at[at], row_send.at[d], row_recv.at[at], lax.rem(me + d, n))

    @pl.loop(1, n)
    def _(d):
        row_copy(d, me).start()

    for k in range(1, BAND + 1):

        @pl.when(me + k >= n)
        def _():
            others[(k - 1) * CB : k * CB] = jnp.zeros((CB, KDIM), jnp.bfloat16)

    rotate(own, lag_ref, turned)

    @pl.when(me + 2 < n)
    def _():
        to_two.wait_recv()
        pl.when(even)(two_up.start)
        pl.when(odd)(two_down.start)

    pair_products(n, turned, own[...], (0,), keeps, corr_ref, None)

    @pl.when(me + 4 < n)
    def _():
        to_four.wait_recv()
        pl.when(even)(four_up.start)

    @pl.when(me + 1 < n)
    def _():
        own_down.wait_recv()

    pair_products(n, turned, others[0 : 2 * CB], (1, 2), keeps, corr_ref, None)

    @pl.loop(1, n)
    def _(d):
        row_copy(d, lax.rem(me + d, n)).wait()

    rows_wide[...] = rows_in[...].astype(jnp.float32)
    for j in range(KDIM // LANES):
        others[BAND * CB :, j * LANES : (j + 1) * LANES] = rows_wide[:, j, :].astype(jnp.bfloat16)

    @pl.when(me + 3 < n)
    def _():
        two_down.wait_recv()

    pair_products(n, turned, others[2 * CB :], (3, 4), keeps, corr_ref, src_ref)

    pl.when(has_low)(to_low.wait_send)
    pl.when(has_high)(to_high.wait_send)
    pl.when(me >= 2)(to_two.wait_send)
    pl.when(me >= 4)(to_four.wait_send)
    pl.when(odd)(own_down.wait_send)

    @pl.when(me + 2 < n)
    def _():
        pl.when(odd)(two_down.wait_send)
        pl.when(even)(two_up.wait_send)

    @pl.when(me + 4 < n)
    def _():
        pl.when(even)(four_up.wait_send)


def per_device(records, filter_taps, segment_ids):
    n = lax.axis_size("fibre")
    me = lax.axis_index("fibre")
    samples = records.shape[1]
    dft, lags = tables()
    seg = jnp.pad(segment_ids.reshape(n, CB), ((1, BAND + 1), (0, 0)), constant_values=-1)
    seg = lax.dynamic_slice_in_dim(seg, me, BAND + 3, 0)
    blocks = -(-samples // TILE)
    vmem = pl.BlockSpec(memory_space=pltpu.VMEM)
    dma = pltpu.SemaphoreType.DMA
    tiles = KDIM // LANES
    corr, src = pl.pallas_call(
        functools.partial(kernel, n),
        out_shape=(
            jax.ShapeDtypeStruct((BAND + 1, CB, LAGS * CB), jnp.bfloat16),
            jax.ShapeDtypeStruct((CB, LAGS * n), jnp.bfloat16),
        ),
        in_specs=[vmem] * 5,
        out_specs=(vmem, vmem),
        scratch_shapes=[
            pltpu.VMEM((16, 2 * LANES), jnp.float32),
            pltpu.VMEM((SPAN * DEPTH, TILE), jnp.bfloat16),
            pltpu.VMEM((CB + 2 * EDGE, LANES), jnp.float32),
            pltpu.VMEM((CB + 2 * EDGE, LANES + blocks * TILE), jnp.float32),
            pltpu.VMEM((blocks * CB, SPAN * DEPTH), jnp.bfloat16),
            pltpu.VMEM((CB, blocks * TILE), jnp.bfloat16),
            pltpu.VMEM((2 * EDGE, samples), jnp.bfloat16),
            pltpu.VMEM((2 * EDGE, samples), jnp.bfloat16),
            pltpu.VMEM((CB, KDIM), jnp.bfloat16),
            pltpu.VMEM((BAND * CB + n, KDIM), jnp.bfloat16),
            pltpu.VMEM((LAGS * CB, KDIM), jnp.bfloat16),
            pltpu.VMEM((tiles, LANES), jnp.float32),
            pltpu.VMEM((tiles, LANES), jnp.bfloat16),
            pltpu.VMEM((n, tiles, LANES), jnp.bfloat16),
            pltpu.VMEM((n, tiles, LANES), jnp.float32),
            dma((2,)),
            dma((2,)),
            dma((4,)),
            dma((BAND,)),
            dma((n,)),
            dma((n,)),
        ],
        compiler_params=pltpu.CompilerParams(
            vmem_limit_bytes=48 << 20, collective_id=0, has_side_effects=True
        ),
        name="correlations",
    )(records, filter_taps, seg, dft, lags)
    return corr.transpose(1, 0, 2), src


def solution(mesh):
    return jax.shard_map(
        per_device,
        mesh=mesh,
        in_specs=(P(("runs", "fibre"), None), P(), P("runs")),
        out_specs=(P(("runs", "fibre"), None, None), P(("runs", "fibre"), None)),
        check_vma=False,
    )
```

```python
import functools

import jax
import jax.numpy as jnp
import numpy as np
from jax import lax
from jax.experimental import pallas as pl
from jax.experimental.pallas import tpu as pltpu
from jax.sharding import PartitionSpec as P

CB = 64
W = 4
F = 200
L = 400
TAPS = 63
SPAN = 9
LAGS = 32
BAND = 4

HALF = SPAN // 2
LANES = 128
PART = 256
WIDE = 2 * PART
PACKED = -(-2 * W * F // LANES) * LANES
TILE = 256
DEPTH = TILE + LANES
EDGE = 8
MESH = pl.DeviceIdType.MESH


def tables():
    time = np.arange(L)
    bins = np.arange(F)
    phase = (time[:, None] * bins[None, :] % L) * (2.0 * np.pi / L)
    taper = 0.5 - 0.5 * np.cos((time + 0.5) * (2.0 * np.pi / L))
    slack = (L % LANES) * (W - 1)
    rows = slack + WIDE
    dft = np.zeros((rows, WIDE), np.float32)
    dft[slack : slack + L, :F] = taper[:, None] * np.cos(phase)
    dft[slack : slack + L, PART : PART + F] = -taper[:, None] * np.sin(phase)
    lag = np.arange(LAGS) - LAGS // 2
    lag_phase = (lag[:, None] * bins[None, :] % L) * (2.0 * np.pi / L)
    scale = 1.0 / np.sqrt(W * F)
    cos, sin = np.cos(lag_phase) * scale, -np.sin(lag_phase) * scale
    lags = np.zeros((2, LAGS, PACKED), np.float32)
    lags[0, :, : 2 * W * F] = np.tile(cos, (1, 2 * W))
    lags[1, :, : 2 * W * F] = np.tile(np.concatenate([sin, -sin], axis=1), (1, W))
    lags = jnp.asarray(lags).astype(jnp.bfloat16).astype(jnp.float32)
    return jnp.asarray(dft).astype(jnp.bfloat16), lags


def column(row):
    across = lax.broadcasted_iota(jnp.int32, (CB, CB), 1)
    down = lax.broadcasted_iota(jnp.int32, (CB, CB), 0)
    return jnp.sum(jnp.where(across == down, row, 0.0), axis=1, keepdims=True)


def build_toeplitz(taps_ref, base, toep):
    base[...] = jnp.zeros_like(base)
    base[0:SPAN, 0:TAPS] = taps_ref[...].astype(jnp.float32)
    toep[...] = jnp.zeros_like(toep)
    for e in range(SPAN):
        rows = jnp.broadcast_to(base[e : e + 1, :], (LANES, 2 * LANES))
        near = pltpu.roll(rows, 0, 1, stride=1, stride_axis=0).astype(jnp.bfloat16)
        at = e * DEPTH
        toep[at : at + LANES, 0:LANES] = near[:, LANES:]
        toep[at + LANES : at + 2 * LANES, :] = near
        toep[at + 2 * LANES : at + 3 * LANES, LANES:] = near[:, :LANES]


def segment_row(seg_ref, block, count):
    per_row = LANES // CB
    at = jnp.clip(block, 0, count - 1)
    line = seg_ref[pl.ds(at // per_row, 1), :].astype(jnp.float32)
    row = line[:, :CB]
    for i in range(1, per_row):
        row = jnp.where(lax.rem(at, per_row) == i, line[:, i * CB : (i + 1) * CB], row)
    return jnp.where((block >= 0) & (block < count), row, -1.0)


def fill_segments(rows, segcol):
    segcol[0:EDGE] = jnp.broadcast_to(column(rows[0])[CB - EDGE :], (EDGE, LANES))
    segcol[EDGE : EDGE + CB] = jnp.broadcast_to(column(rows[1]), (CB, LANES))
    segcol[EDGE + CB :] = jnp.broadcast_to(column(rows[2])[:EDGE], (EDGE, LANES))


def filter_and_transform(xf, segcol, xs, toep, y, dft_ref):
    blocks = xs.shape[0] // CB
    own = segcol[EDGE : EDGE + CB]
    for e in range(SPAN):
        lower = EDGE - HALF + e
        keep = segcol[lower : lower + CB] == own
        for j in range(xf.shape[1] // LANES):
            part = xf[lower : lower + CB, j * LANES : (j + 1) * LANES]
            part = jnp.where(keep, part, 0.0).astype(jnp.bfloat16)
            for b in range(blocks):
                k = j - b * (TILE // LANES)
                if 0 <= k < DEPTH // LANES:
                    at = e * DEPTH + k * LANES
                    xs[b * CB : (b + 1) * CB, at : at + LANES] = part
    out = jnp.dot(xs[...], toep[...], preferred_element_type=jnp.float32)
    out = out.astype(jnp.bfloat16)
    for b in range(blocks):
        y[:, b * TILE : (b + 1) * TILE] = out[b * CB : (b + 1) * CB]
    slack = L % LANES
    packed, swapped = [], []
    for w in range(W):
        first = w * (L - slack)
        top = slack * (W - 1 - w)
        raw = jnp.dot(
            y[:, first : first + WIDE],
            dft_ref[top : top + WIDE, :],
            preferred_element_type=jnp.float32,
        )
        power = jnp.sum(raw * raw, axis=-1, keepdims=True) * (1.0 / (2 * F))
        value = raw * lax.rsqrt(power + 1e-06)
        re, im = value[:, :F], value[:, PART : PART + F]
        packed += [re, im]
        swapped += [im, re]
    tail = [jnp.zeros((CB, PACKED - 2 * W * F), jnp.float32)]
    return jnp.concatenate(packed + tail, axis=1), jnp.concatenate(swapped + tail, axis=1)


def rotate(own_ref, swapped_ref, lag_ref, turned):
    middle = LAGS // 2
    for lower in range(0, PACKED, LANES):
        lanes = slice(lower, lower + LANES)
        own = own_ref[:, lanes].astype(jnp.float32)
        swapped = swapped_ref[:, lanes].astype(jnp.float32)
        for l in range(middle + 1):
            a, b = own * lag_ref[0, l : l + 1, lanes], swapped * lag_ref[1, l : l + 1, lanes]
            turned[l * CB : (l + 1) * CB, lanes] = (a + b).astype(jnp.bfloat16)
            if 0 < l < middle:
                back = 2 * middle - l
                turned[back * CB : (back + 1) * CB, lanes] = (a - b).astype(jnp.bfloat16)


def place(total, lags, first, blocks, keeps, corr_ref, n, src_ref):
    def at(l, lower, width):
        return total[(l - first) * CB : (l - first + 1) * CB, lower : lower + width]

    for l in range(first, first + lags, 2):
        for i, k in enumerate(blocks):
            pair = jnp.concatenate([at(l, i * CB, CB), at(l + 1, i * CB, CB)], axis=1)
            pair = jnp.where(keeps[k], pair, 0.0)
            corr_ref[k, :, l * CB : (l + 2) * CB] = pair.astype(jnp.bfloat16)
    if src_ref is None:
        return
    lower = len(blocks) * CB
    gathers = jnp.concatenate([at(l, lower, n) for l in range(first, first + lags)], axis=1)
    src_ref[:, first * n : (first + lags) * n] = gathers.astype(jnp.bfloat16)


def pair_masks(rows):
    own = jnp.broadcast_to(column(rows[1]), (CB, 2 * CB))
    return [own == jnp.concatenate([row, row], axis=1) for row in rows[1:]]


def pair_products(n, turned, partner, blocks, keeps, corr_ref, src_ref):
    group = 8
    for first in range(0, LAGS, group):
        total = lax.dot_general(
            turned[first * CB : (first + group) * CB],
            partner,
            (((1,), (1,)), ((), ())),
            preferred_element_type=jnp.float32,
        )
        place(total, group, first, blocks, keeps, corr_ref, n, src_ref)


def kernel(
    n, taps_ref, x_hbm, seg_hbm, dft_hbm, lag_hbm, corr_ref, src_ref,
    x_ref, seg_ref, dft_ref, lag_ref,
    base, toep, segcol, xf, xs, y, low, high, own, swapped, others, turned,
    row, row_tile, rows_in, rows_wide,
    load_sem, halo_send, halo_recv, block_send, block_recv, row_send, row_recv,
):
    me = lax.axis_index("fibre")
    loads = [
        pltpu.make_async_copy(source, target, load_sem.at[i])
        for i, (source, target) in enumerate(
            [(x_hbm, x_ref), (seg_hbm, seg_ref), (dft_hbm, dft_ref), (lag_hbm, lag_ref)]
        )
    ]
    for load in loads:
        load.start()
    barrier = pltpu.get_barrier_semaphore()

    @pl.loop(1, n)
    def _(d):
        pl.semaphore_signal(barrier, inc=1, device_id={"fibre": lax.rem(me + d, n)}, device_id_type=MESH)

    build_toeplitz(taps_ref, base, toep)
    xf[...] = jnp.zeros_like(xf)
    loads[1].wait()
    seg_rows = [segment_row(seg_ref, me + k, n) for k in range(-1, BAND + 1)]
    fill_segments(seg_rows, segcol)
    keeps = pair_masks(seg_rows)
    loads[0].wait()
    samples = x_ref.shape[1]
    xf[EDGE : EDGE + CB, LANES : LANES + samples] = x_ref[...].astype(jnp.float32)
    halo = low.shape[0]
    pl.semaphore_wait(barrier, n - 1)

    def remote(source, target, send, recv, device):
        return pltpu.make_async_remote_copy(
            src_ref=source, dst_ref=target, send_sem=send, recv_sem=recv,
            device_id={"fibre": device}, device_id_type=MESH,
        )

    has_low, has_high = me > 0, me < n - 1
    to_low = remote(x_ref.at[0:halo], high, halo_send.at[0], halo_recv.at[0], me - 1)
    to_high = remote(x_ref.at[CB - halo : CB], low, halo_send.at[1], halo_recv.at[1], me + 1)
    pl.when(has_low)(to_low.start)
    pl.when(has_high)(to_high.start)

    @pl.when(has_high)
    def _():
        to_low.wait_recv()
        xf[EDGE + CB :, LANES : LANES + samples] = high[0:EDGE].astype(jnp.float32)

    @pl.when(has_low)
    def _():
        to_high.wait_recv()
        xf[0:EDGE, LANES : LANES + samples] = low[halo - EDGE :].astype(jnp.float32)

    loads[2].wait()
    value, turned_value = filter_and_transform(xf, segcol, xs, toep, y, dft_ref)
    own[...] = value.astype(jnp.bfloat16)
    swapped[...] = turned_value.astype(jnp.bfloat16)
    for j in range(PACKED // LANES):
        row[j : j + 1, :] = value[0:1, j * LANES : (j + 1) * LANES]

    def slot(k):
        return others.at[(k - 1) * CB : k * CB]

    def block_copy(source, k, sem, device):
        return remote(source, slot(k), block_send.at[sem], block_recv.at[k - 1], device)

    even = lax.rem(me, 2) == 0
    odd = lax.rem(me, 2) == 1
    to_two = block_copy(own, 2, 0, me - 2)
    to_four = block_copy(own, 4, 1, me - 4)
    own_down = block_copy(own, 1, 2, me - 1)
    two_down = block_copy(slot(2), 3, 3, me - 1)
    two_up = block_copy(slot(2), 1, 2, me + 1)
    four_up = block_copy(slot(4), 3, 3, me + 1)
    pl.when(me >= 2)(to_two.start)
    pl.when(me >= 4)(to_four.start)
    pl.when(odd)(own_down.start)
    row[PACKED // LANES :, :] = jnp.zeros((row.shape[0] - PACKED // LANES, LANES), jnp.float32)
    row_tile[...] = row[...].astype(jnp.bfloat16)
    rows_in[me] = row_tile[...]

    def row_copy(d, at):
        return remote(row_tile, rows_in.at[at], row_send.at[d], row_recv.at[at], lax.rem(me + d, n))

    @pl.loop(1, n)
    def _(d):
        row_copy(d, me).start()

    for k in range(1, BAND + 1):

        @pl.when(me + k >= n)
        def _():
            others[(k - 1) * CB : k * CB] = jnp.zeros((CB, PACKED), jnp.bfloat16)

    loads[3].wait()
    rotate(own, swapped, lag_ref, turned)

    @pl.when(me + 2 < n)
    def _():
        to_two.wait_recv()
        pl.when(even)(two_up.start)
        pl.when(odd)(two_down.start)

    pair_products(n, turned, own[...], (0,), keeps, corr_ref, None)

    @pl.when(me + 4 < n)
    def _():
        to_four.wait_recv()
        pl.when(even)(four_up.start)

    @pl.when(me + 1 < n)
    def _():
        own_down.wait_recv()

    pair_products(n, turned, others[0 : 2 * CB], (1, 2), keeps, corr_ref, None)

    @pl.loop(1, n)
    def _(d):
        row_copy(d, lax.rem(me + d, n)).wait()

    rows_wide[...] = rows_in[...].astype(jnp.float32)
    for j in range(PACKED // LANES):
        others[BAND * CB :, j * LANES : (j + 1) * LANES] = rows_wide[:, j, :].astype(jnp.bfloat16)

    @pl.when(me + 3 < n)
    def _():
        two_down.wait_recv()

    pair_products(n, turned, others[2 * CB :], (3, 4), keeps, corr_ref, src_ref)

    pl.when(has_low)(to_low.wait_send)
    pl.when(has_high)(to_high.wait_send)
    pl.when(me >= 2)(to_two.wait_send)
    pl.when(me >= 4)(to_four.wait_send)
    pl.when(odd)(own_down.wait_send)

    @pl.when(me + 2 < n)
    def _():
        pl.when(odd)(two_down.wait_send)
        pl.when(even)(two_up.wait_send)

    @pl.when(me + 4 < n)
    def _():
        pl.when(even)(four_up.wait_send)


def per_device(records, filter_taps, segment_ids):
    n = lax.axis_size("fibre")
    samples = records.shape[1]
    dft, lags = tables()
    seg = segment_ids.reshape(-1, LANES)
    blocks = -(-samples // TILE)
    vmem = pl.BlockSpec(memory_space=pltpu.VMEM)
    dma = pltpu.SemaphoreType.DMA
    hbm = pl.BlockSpec(memory_space=pltpu.HBM)
    tiles = -(-PACKED // LANES // 16) * 16
    corr, src = pl.pallas_call(
        functools.partial(kernel, n),
        out_shape=(
            jax.ShapeDtypeStruct((BAND + 1, CB, LAGS * CB), jnp.bfloat16),
            jax.ShapeDtypeStruct((CB, LAGS * n), jnp.bfloat16),
        ),
        in_specs=[vmem] + [hbm] * 4,
        out_specs=(vmem, vmem),
        scratch_shapes=[
            pltpu.VMEM(records.shape, records.dtype),
            pltpu.VMEM(seg.shape, seg.dtype),
            pltpu.VMEM(dft.shape, dft.dtype),
            pltpu.VMEM(lags.shape, lags.dtype),
            pltpu.VMEM((16, 2 * LANES), jnp.float32),
            pltpu.VMEM((SPAN * DEPTH, TILE), jnp.bfloat16),
            pltpu.VMEM((CB + 2 * EDGE, LANES), jnp.float32),
            pltpu.VMEM((CB + 2 * EDGE, LANES + blocks * TILE), jnp.float32),
            pltpu.VMEM((blocks * CB, SPAN * DEPTH), jnp.bfloat16),
            pltpu.VMEM((CB, blocks * TILE), jnp.bfloat16),
            pltpu.VMEM((2 * EDGE, samples), jnp.bfloat16),
            pltpu.VMEM((2 * EDGE, samples), jnp.bfloat16),
            pltpu.VMEM((CB, PACKED), jnp.bfloat16),
            pltpu.VMEM((CB, PACKED), jnp.bfloat16),
            pltpu.VMEM((BAND * CB + n, PACKED), jnp.bfloat16),
            pltpu.VMEM((LAGS * CB, PACKED), jnp.bfloat16),
            pltpu.VMEM((tiles, LANES), jnp.float32),
            pltpu.VMEM((tiles, LANES), jnp.bfloat16),
            pltpu.VMEM((n, tiles, LANES), jnp.bfloat16),
            pltpu.VMEM((n, tiles, LANES), jnp.float32),
            dma((4,)),
            dma((2,)),
            dma((2,)),
            dma((4,)),
            dma((BAND,)),
            dma((n,)),
            dma((n,)),
        ],
        compiler_params=pltpu.CompilerParams(
            vmem_limit_bytes=62 << 20, collective_id=0, has_side_effects=True
        ),
        name="correlations",
    )(filter_taps, records, seg, dft, lags)
    return corr.transpose(1, 0, 2), src


def solution(mesh):
    return jax.shard_map(
        per_device,
        mesh=mesh,
        in_specs=(P(("runs", "fibre"), None), P(), P("runs")),
        out_specs=(P(("runs", "fibre"), None, None), P(("runs", "fibre"), None)),
        check_vma=False,
    )
```
